32 devices in a mesh: dp: 2 (over core), section: 4 (over y, x), expert: 4 (over z).
Axes of the slice: x: 2, y: 2, z: 4, core: 2. Of those that a mesh axis runs over, the one named last changes fastest.
Arguments:
- grad_out: bfloat16 [1024, 3584], P(('dp', 'expert'), 'section'), may hold values from -6 to 6
- expert_ids: int32 [1024, 8], P(('dp', 'expert')), may hold values from 0 to 63, all different within a row; in each aligned block of 128 rows (0 to 127, 128 to 255, ...) at most 24 rows name the same one
- gate_weights: float32 [1024, 8], P(('dp', 'expert')), may hold values from 0.1 to 1
- act: bfloat16 [1024, 8, 1024], P(('dp', 'expert'), None, 'section'), may hold values from -0.8984375 to 0.8984375
- w_down: bfloat16 [64, 1024, 3584], P('expert', 'section'), may hold values from -0.09375 to 0.09375
Outputs:
- grad_hidden: bfloat16 [1024, 8, 1024], P(('dp', 'expert'), None, 'section')
- grad_gates: float32 [1024, 8], P(('dp', 'expert'))
- grad_w: bfloat16 [64, 1024, 3584], P('expert', 'section', 'dp')
The draws below stay inside these ranges and needn't reach their ends.
Inputs may be any that keep to these rules, and one draw needn't show every extreme that they name: `expert_ids`: each row names 8 different experts. In each aligned block of 128 rows (the tokens of one device) no expert is named by more than 24 rows, and in every draw some expert is named by exactly 24 rows of some block.
All inputs are finite; a program needn't handle non-finite values.
Results may differ from the reference program's by a relative error of at most 0.0058.
Values may be sent and summed in bfloat16 or wider, within the bound.
A program may use at most 128 MiB of HBM per device.

```python
import math
import jax
import jax.numpy as jnp
import numpy as np
from jax import lax

D = 3584
H = 1024
K = 8
TOK_DEV = 128
EXPERTS = 64
SLOT = 24
ROWS = 96
TOKENS = 1024
N_DP = 2
N_EXPERT = 4


def block_scale(rng, dims, shards, low, high):
    level, own = 1.0, jax.random.fold_in(rng, 6)
    for dim, shards_of in shards:
        steps = jnp.exp(jax.random.uniform(jax.random.fold_in(own, dim), (shards_of,), jnp.float32, low / len(shards), high / len(shards)))
        level = level * jnp.repeat(steps, dims[dim] // shards_of).reshape([-1 if axis == dim else 1 for axis in range(len(dims))])
    return level


def assign_block(stream_key, own, number, rows, amount, top, limit, lean):
    ranking = jax.random.permutation(stream_key, amount)
    heavy_load, common = shares(amount, rows * top, limit, lean, True), shares(amount, rows * top, limit, lean, False)
    places = jnp.arange(amount)

    def named(sizes, turn):
        used = int((sizes > 0).sum())
        fixed = max(1, used // 4)
        moved = fixed + (places - fixed + turn * (used - fixed)) % max(1, amount - fixed)
        return jnp.zeros((amount,), jnp.int32).at[ranking[jnp.where(places < fixed, places, moved)]].set(jnp.asarray(sizes, jnp.int32))

    sizes = jnp.where(number % 4 == 0, named(heavy_load, number // 4), named(common, number - number // 4 - 1))
    mixed = jax.random.permutation(jax.random.fold_in(own, 3), amount)
    source_of, taker = mixed[0:amount // 2 * 2:2], mixed[1:amount // 2 * 2:2]
    margin = jnp.minimum(sizes[source_of] - 1, limit - sizes[taker]) // 2
    margin = jnp.where((source_of == ranking[0]) | (taker == ranking[0]) | (sizes[taker] == 0), 0, jnp.maximum(margin, 0))
    moved = jax.random.randint(jax.random.fold_in(own, 4), (amount // 2,), 0, 1 << 20) % (margin + 1)
    sizes = sizes.at[source_of].add(-moved).at[taker].add(moved)
    members = jnp.searchsorted(jnp.cumsum(sizes), jnp.arange(rows * top), side="right").astype(jnp.int32)
    listing = members.reshape(top, rows).T
    listing = listing[jax.random.permutation(jax.random.fold_in(own, 1), rows)]
    turn = jax.random.randint(jax.random.fold_in(own, 2), (rows, 1), 0, top)
    return jnp.take_along_axis(listing, (jnp.arange(top)[None, :] + turn) % top, axis=1)


def shares(amount, total, reach, lean, full):
    weights = [(1 << 20) // math.isqrt(rank ** lean) + 1 for rank in range(1, amount + 1)]
    largest = reach if full else min(reach, max(-(-total // amount), total * weights[0] // sum(weights)))
    least = 1 if total - largest >= amount - 1 else 0
    given, surplus = [largest] + [least] * (amount - 1), total - largest - least * (amount - 1)
    while surplus > 0:
        candidates = [i for i in range(1, amount) if given[i] < largest] or [i for i in range(1, amount) if given[i] < reach]
        pool, budget = sum([weights[i] for i in candidates]), surplus
        for i in candidates:
            more = min(reach - given[i], max(1, budget * weights[i] // pool), surplus)
            given[i] = given[i] + more
            surplus = surplus - more
    return np.array(given)


def gaussian(rng, extent, spread, most, pieces=(), kind=jnp.bfloat16):
    result = jax.random.normal(rng, extent, jnp.float32) * spread
    if len(pieces) > 0:
        result = block_scale(rng, extent, pieces, -0.22, 0.18) * result
    return jnp.clip(result, min=-most, max=most).astype(kind)


def setup_inputs(seed: int = 0) -> dict:
    arg_keys = jax.random.split(jax.random.key(seed), 6)
    grad_out = gaussian(arg_keys[0], (TOKENS, D), 1.0, 6.0, ((0, 8), (1, 4)))
    expert_ids_keys = jax.random.split(jax.random.fold_in(arg_keys[1], 1), TOKENS // TOK_DEV)
    expert_ids_turns = jax.random.permutation(jax.random.fold_in(arg_keys[1], 3), TOKENS // TOK_DEV)
    expert_ids = jax.vmap(lambda own, number: assign_block(jax.random.fold_in(arg_keys[1], 2), own, number, TOK_DEV, EXPERTS, K, SLOT, 2))(expert_ids_keys, expert_ids_turns).reshape((TOKENS, K))
    gate_weights = jnp.clip(jnp.exp(math.log(1.0) - 2.3025851 * jax.random.uniform(arg_keys[2], (TOKENS, K), jnp.float32) ** block_scale(arg_keys[2], (TOKENS, K), ((0, 8),), -0.2, 0.2)), 0.1, 1.0)
    act = gaussian(arg_keys[3], (TOKENS, K, H), 0.15, 0.8984375, ((0, 8), (2, 4)))
    w_down = gaussian(arg_keys[4], (EXPERTS, H, D), D ** -0.5, 0.09375, ((0, 4), (1, 4)))
    return {"grad_out": grad_out, "expert_ids": expert_ids, "gate_weights": gate_weights, "act": act, "w_down": w_down}


def reference(grad_out, expert_ids, gate_weights, act, w_down):
    per_replica = TOK_DEV * N_EXPERT
    pair_count = per_replica * K
    scaled = (gate_weights[:, :, None] * act.astype(jnp.float32)).astype(jnp.bfloat16)
    unscaled_parts = []
    weight_total = jnp.zeros((EXPERTS, H, D), jnp.float32)
    for replica in range(N_DP):
        grad_rep = grad_out[replica * per_replica:(replica + 1) * per_replica]
        scaled_rep = scaled[replica * per_replica:(replica + 1) * per_replica]
        targets = expert_ids[replica * per_replica:(replica + 1) * per_replica].reshape(pair_count)
        ordering = jnp.argsort(targets, stable=True).astype(jnp.int32)
        counts = jnp.sum((targets[:, None] == jnp.arange(EXPERTS, dtype=jnp.int32)[None, :]).astype(jnp.int32), axis=0)
        offsets = (jnp.cumsum(counts) - counts).astype(jnp.int32)
        ordering_ext = jnp.concatenate([ordering, jnp.zeros((ROWS,), jnp.int32)])
        chosen_all = ordering_ext[offsets[:, None] + jnp.arange(ROWS, dtype=jnp.int32)[None, :]]
        filled_all = jnp.arange(ROWS, dtype=jnp.int32)[None, :] < counts[:, None]

        def expert_terms(expert):
            chosen = chosen_all[expert]
            filled = filled_all[expert]
            token_at = chosen // K
            route_at = chosen % K
            grad_rows = jnp.where(filled[:, None], grad_rep[token_at], jnp.zeros((), grad_rep.dtype))
            scaled_rows = jnp.where(filled[:, None], scaled_rep[token_at, route_at], jnp.zeros((), scaled_rep.dtype))
            unscaled_rows = jnp.dot(grad_rows, w_down[expert].T, preferred_element_type=jnp.float32)
            weight_part = jnp.dot(scaled_rows.T, grad_rows, preferred_element_type=jnp.float32)
            return unscaled_rows.astype(jnp.bfloat16), weight_part.astype(jnp.bfloat16)

        unscaled_all, weight_parts = lax.map(expert_terms, jnp.arange(EXPERTS, dtype=jnp.int32))
        scatter_at = jnp.where(filled_all, chosen_all, pair_count).reshape(-1)
        unscaled_pairs = jnp.zeros((pair_count, H), jnp.bfloat16).at[scatter_at].set(unscaled_all.reshape(-1, H), mode="drop")
        unscaled_parts.append(unscaled_pairs.reshape(per_replica, K, H))
        weight_total = weight_total + weight_parts.astype(jnp.float32)
    unscaled = jnp.concatenate(unscaled_parts, axis=0)
    grad_hidden = (gate_weights[:, :, None] * unscaled.astype(jnp.float32)).astype(jnp.bfloat16)
    grad_gates = jnp.sum(act.astype(jnp.float32) * unscaled.astype(jnp.float32), axis=2)
    return grad_hidden, grad_gates, weight_total.astype(jnp.bfloat16)
```

```python
import functools

import jax
import jax.numpy as jnp
from jax import lax
from jax.experimental import pallas as pl
from jax.experimental.pallas import tpu as pltpu
from jax.sharding import PartitionSpec as P

BF = jnp.bfloat16
F32 = jnp.float32
MESH = pl.DeviceIdType.MESH


def slots_of(expert_ids, experts, capacity):
    tok_count = expert_ids.shape[0]
    onehot = expert_ids[:, :, None] == jnp.arange(experts, dtype=jnp.int32)
    named = jnp.any(onehot, axis=1).astype(BF)
    earlier = jnp.arange(tok_count)[:, None] > jnp.arange(tok_count)[None, :]
    before = jnp.dot(earlier.astype(BF), named, preferred_element_type=F32)
    order_in = jnp.sum(jnp.where(onehot, before[:, None, :], 0.0), axis=2).astype(jnp.int32)
    return expert_ids * capacity + order_in


def arrange(received, n_expert, exp_dev):
    capacity = received.shape[1]
    width = received.shape[2]
    grouped = received.reshape(n_expert, exp_dev, capacity, width)
    return jnp.transpose(grouped, (1, 0, 2, 3)).reshape(exp_dev, n_expert * capacity, width)


def local_general(grad_out, expert_ids, gate_weights, act, w_down):
    tok_count, top_count = expert_ids.shape
    hidden_slice = act.shape[2]
    exp_dev = w_down.shape[0]
    n_expert = lax.axis_size("expert")
    experts = exp_dev * n_expert
    capacity = 3 * tok_count * top_count // (2 * experts)
    pair_count = tok_count * top_count
    position = slots_of(expert_ids, experts, capacity).reshape(pair_count)
    source = (
        jnp.full((experts * capacity,), pair_count, jnp.int32)
        .at[position]
        .set(jnp.arange(pair_count, dtype=jnp.int32))
    )
    filled = source < pair_count
    token_index = jnp.where(filled, source // top_count, tok_count)
    scaled = (
        (gate_weights[:, :, None] * act.astype(F32)).astype(BF).reshape(pair_count, hidden_slice)
    )
    scaled_ext = jnp.concatenate([scaled, jnp.zeros((1, hidden_slice), BF)], axis=0)
    send_scaled = scaled_ext[jnp.where(filled, source, pair_count)].reshape(
        experts, capacity, hidden_slice
    )
    full_rows = lax.all_gather(grad_out, "section", axis=1, tiled=True)
    rows_ext = jnp.concatenate([full_rows, jnp.zeros((1, full_rows.shape[1]), BF)], axis=0)
    send_grad = rows_ext[token_index].reshape(experts, capacity, full_rows.shape[1])
    recv_grad, recv_scaled = (
        lax.all_to_all(send_grad, "expert", split_axis=0, concat_axis=0, tiled=True),
        lax.all_to_all(send_scaled, "expert", split_axis=0, concat_axis=0, tiled=True),
    )
    recv_grad = arrange(recv_grad, n_expert, exp_dev)
    recv_scaled = arrange(recv_scaled, n_expert, exp_dev)
    unscaled = jnp.einsum("erd,ehd->erh", recv_grad, w_down, preferred_element_type=F32)
    weight_part = jnp.einsum("erh,erd->ehd", recv_scaled, recv_grad, preferred_element_type=F32)
    grad_w = lax.psum_scatter(weight_part.astype(BF), "dp", scatter_dimension=2, tiled=True)
    returning = unscaled.astype(BF).reshape(exp_dev, n_expert, capacity, hidden_slice)
    returning = jnp.transpose(returning, (1, 0, 2, 3)).reshape(experts, capacity, hidden_slice)
    returned = lax.all_to_all(returning, "expert", split_axis=0, concat_axis=0, tiled=True)
    unscaled_tok = returned.reshape(experts * capacity, hidden_slice)[position].reshape(
        tok_count, top_count, hidden_slice
    )
    grad_hidden = (gate_weights[:, :, None] * unscaled_tok.astype(F32)).astype(BF)
    gate_share = jnp.sum(act.astype(F32) * unscaled_tok.astype(F32), axis=2)
    return (grad_hidden, lax.psum(gate_share, "section"), grad_w)


def spread(
    g_ref, ids_ref, s_ref, g_all, g_half, ids_all, s_all, here,
    a_snd, a_rcv, x_snd, x_rcv, y_snd, y_rcv, d_snd, d_rcv, h_snd, h_rcv,
    s_snd, s_rcv, f_snd, f_rcv, i_snd, i_rcv,
):
    dp, sec, z = (lax.axis_index(a) for a in ("dp", "section", "expert"))
    width = g_ref.shape[1]
    half = g_half.shape[2]
    mate = 1 - dp
    sx = sec + 1 - 2 * (sec % 2)
    sy = (sec + 2) % 4
    to_mate, to_x, to_y = (mate, sec, z), (dp, sx, z), (dp, sy, z)
    to_z = [(dp, sec, (z + j) % 4) for j in range(4)]
    other = [(mate, sec, (z + j) % 4) for j in range(4)]
    peers = [to_mate, to_x, to_y] + to_z[1:] + other[1:]

    barrier = pltpu.get_barrier_semaphore()
    for peer in peers:
        pl.semaphore_signal(barrier, inc=1, device_id=peer, device_id_type=MESH)
    pl.semaphore_wait(barrier, len(peers))

    def send(src, dst, snd, rcv, to):
        copy = pltpu.make_async_remote_copy(
            src_ref=src, dst_ref=dst, send_sem=snd, recv_sem=rcv, device_id=to, device_id_type=MESH
        )
        copy.start()
        return copy

    def cols(s):
        return pl.ds(pl.multiple_of(s * width, 128), width)

    zs = [(z + 4 - j) % 4 for j in range(4)]

    def shard(j, s):
        return g_all.at[zs[j], :, cols(s)]

    order = (1, 3, 2)
    a = {j: send(g_ref, shard(0, sec), a_snd.at[j], a_rcv.at[j], to_z[j]) for j in order}
    x = {0: send(g_ref, shard(0, sec), x_snd.at[0], x_rcv.at[0], to_x)}
    y = {0: send(g_ref, shard(0, sec), y_snd.at[0], y_rcv.at[0], to_y)}
    own = [
        pltpu.make_async_copy(g_ref, shard(0, sec), here.at[0]),
        pltpu.make_async_copy(ids_ref, ids_all.at[dp, z], here.at[1]),
        pltpu.make_async_copy(s_ref.at[z], s_all.at[dp, z], here.at[2]),
    ]
    for c in own:
        c.start()
    ids = [send(ids_ref, ids_all.at[dp, z], i_snd.at[0, 0], i_rcv.at[0, 0], to_mate)]
    for j in order:
        ids.append(send(ids_ref, ids_all.at[dp, z], i_snd.at[0, j], i_rcv.at[0, j], to_z[j]))
        ids.append(send(ids_ref, ids_all.at[dp, z], i_snd.at[1, j], i_rcv.at[1, j], other[j]))

    for j in order:
        a[j].wait_recv()
        x[j] = send(shard(j, sec), shard(j, sec), x_snd.at[j], x_rcv.at[j], to_x)
        y[j] = send(shard(j, sec), shard(j, sec), y_snd.at[j], y_rcv.at[j], to_y)
    s = {
        j: send(s_ref.at[(z + j) % 4], s_all.at[dp, z], s_snd.at[j], s_rcv.at[j], to_z[j])
        for j in order
    }
    d = {}
    for j in (0,) + order:
        if j % 2 == 0:
            x[j].wait_recv()
            d[j] = send(shard(j, sx), shard(j, sx), d_snd.at[j], d_rcv.at[j], to_y)
        else:
            y[j].wait_recv()
            d[j] = send(shard(j, sy), shard(j, sy), d_snd.at[j], d_rcv.at[j], to_x)
    for c in own:
        c.wait()
    h, f = [], []
    f.append(send(s_all.at[dp, z], s_all.at[dp, z], f_snd.at[0], f_rcv.at[0], to_mate))
    mate_cols = pl.ds(pl.multiple_of(mate * half, 128), half)
    for j in (0,) + order:
        (y if j % 2 == 0 else x)[j].wait_recv()
        d[j].wait_recv()
        h.append(
            send(g_all.at[zs[j], :, mate_cols], g_half.at[zs[j]], h_snd.at[j], h_rcv.at[j], to_mate)
        )
    for j in order:
        s[j].wait_recv()
        f.append(
            send(s_all.at[dp, zs[j]], s_all.at[dp, zs[j]], f_snd.at[j], f_rcv.at[j], to_mate)
        )
    for c in ids + h + f:
        c.wait_recv()
    for c in [*a.values(), *x.values(), *y.values(), *d.values(), *s.values(), *ids, *h, *f]:
        c.wait_send()


def spread_call(grad_out, ids_t, send_scaled):
    tok_count, width = grad_out.shape
    shapes = (
        jax.ShapeDtypeStruct((4, tok_count, 4 * width), BF),
        jax.ShapeDtypeStruct((4, tok_count, 2 * width), BF),
        jax.ShapeDtypeStruct((2, 4) + ids_t.shape, jnp.int32),
        jax.ShapeDtypeStruct((2,) + send_scaled.shape, BF),
    )
    vmem = pl.BlockSpec(memory_space=pltpu.VMEM)
    sems = [pltpu.SemaphoreType.DMA((4,))] * 14
    return pl.pallas_call(
        spread,
        out_shape=shapes,
        in_specs=[vmem] * 3,
        out_specs=(vmem,) * 4,
        scratch_shapes=[pltpu.SemaphoreType.DMA((3,))] + sems + [pltpu.SemaphoreType.DMA((2, 4))] * 2,
        compiler_params=pltpu.CompilerParams(
            collective_id=0, has_side_effects=True, vmem_limit_bytes=24 * 2**20
        ),
    )(grad_out, ids_t, send_scaled)


def local(grad_out, expert_ids, gate_weights, act, w_down):
    tok_count, top_count = expert_ids.shape
    hidden = act.shape[2]
    exp_dev = w_down.shape[0]
    experts = exp_dev * 4
    capacity = 3 * tok_count * top_count // (2 * experts)
    pairs = tok_count * top_count
    dp, z = lax.axis_index("dp"), lax.axis_index("expert")

    position = slots_of(expert_ids, experts, capacity).reshape(pairs)
    scaled = (gate_weights[:, :, None] * act.astype(F32)).astype(BF).reshape(pairs, hidden)
    slots = jnp.arange(experts * capacity, dtype=jnp.int32)
    place = (slots[:, None] == position[None, :]).astype(BF)
    send_scaled = jnp.dot(place, scaled, preferred_element_type=F32).astype(BF)
    send_scaled = send_scaled.reshape(4, exp_dev * capacity, hidden)

    g_all, g_half, ids_all, s_all = spread_call(grad_out, expert_ids.T, send_scaled)

    mine = z * exp_dev + jnp.arange(exp_dev, dtype=jnp.int32)
    named = jnp.any(ids_all[:, :, None] == mine[None, None, :, None, None], axis=3)
    earlier = jnp.arange(tok_count)[:, None] < jnp.arange(tok_count)[None, :]
    before = jnp.einsum(
        "rseu,ut->rset", named.astype(BF), earlier.astype(BF), preferred_element_type=F32
    ).astype(jnp.int32)
    before = jnp.where(named, before, -1)
    pick = (before[:, :, :, None, :] == jnp.arange(capacity)[:, None]).astype(BF)

    def rows_of(chosen, table):
        rows = jnp.einsum("sect,std->escd", chosen, table, preferred_element_type=F32)
        return rows.astype(BF).reshape(exp_dev, 4 * capacity, table.shape[2])

    pick_own = lax.dynamic_index_in_dim(pick, dp, 0, keepdims=False)
    pick_mate = lax.dynamic_index_in_dim(pick, 1 - dp, 0, keepdims=False)
    rows = rows_of(pick_own, g_all)
    half = g_half.shape[2]
    rows_half = lax.dynamic_slice_in_dim(rows, dp * half, half, 2)
    rows_mate = rows_of(pick_mate, g_half)

    unscaled = jnp.einsum("erd,ehd->erh", rows, w_down, preferred_element_type=F32).astype(BF)
    returning = jnp.transpose(unscaled.reshape(exp_dev, 4, capacity, hidden), (1, 0, 2, 3))
    back = []
    for j in range(4):
        block = lax.dynamic_index_in_dim(returning, (z + j) % 4, 0, keepdims=False)
        block = block.reshape(exp_dev * capacity, hidden)
        if j:
            block = lax.ppermute(block, "expert", [(i, (i + j) % 4) for i in range(4)])
        back.append(block)

    def by_expert(index):
        part = lax.dynamic_index_in_dim(s_all, index, 0, keepdims=False)
        part = part.reshape(4, exp_dev, capacity, hidden)
        return jnp.transpose(part, (1, 0, 2, 3)).reshape(exp_dev, 4 * capacity, hidden)

    scaled_rows = jnp.concatenate([by_expert(dp), by_expert(1 - dp)], axis=1)
    both = jnp.concatenate([rows_half, rows_mate], axis=1)
    grad_w = jnp.einsum("erh,erd->ehd", scaled_rows, both, preferred_element_type=F32).astype(BF)

    per_dev = exp_dev * capacity
    at = (z + 4 - position // per_dev) % 4 * per_dev + position % per_dev
    fetch = (at[:, None] == slots[None, :]).astype(BF)
    unscaled_tok = jnp.dot(fetch, jnp.concatenate(back, axis=0), preferred_element_type=F32)
    unscaled_tok = unscaled_tok.reshape(tok_count, top_count, hidden)
    grad_hidden = (gate_weights[:, :, None] * unscaled_tok).astype(BF)
    gate_share = jnp.sum(act.astype(F32) * unscaled_tok, axis=2)
    return (grad_hidden, lax.psum(gate_share, "section"), grad_w)


def solution(mesh):
    placed = (
        P(("dp", "expert"), "section"),
        P(("dp", "expert"), None),
        P(("dp", "expert"), None),
        P(("dp", "expert"), None, "section"),
        P("expert", "section", None),
    )
    sizes = tuple(mesh.shape[a] for a in ("dp", "section", "expert"))
    return jax.shard_map(
        local if sizes == (2, 4, 4) else local_general,
        mesh=mesh,
        in_specs=placed,
        out_specs=(
            P(("dp", "expert"), None, "section"),
            P(("dp", "expert"), None),
            P("expert", "section", "dp"),
        ),
        check_vma=False,
    )
```

```python
import functools

import jax
import jax.numpy as jnp
from jax import lax
from jax.experimental import pallas as pl
from jax.experimental.pallas import tpu as pltpu
from jax.sharding import PartitionSpec as P

BF = jnp.bfloat16
F32 = jnp.float32
MESH = pl.DeviceIdType.MESH


def slots_of(expert_ids, experts, capacity):
    tok_count = expert_ids.shape[0]
    onehot = expert_ids[:, :, None] == jnp.arange(experts, dtype=jnp.int32)
    named = jnp.any(onehot, axis=1).astype(BF)
    earlier = jnp.arange(tok_count)[:, None] > jnp.arange(tok_count)[None, :]
    before = jnp.dot(earlier.astype(BF), named, preferred_element_type=F32)
    order_in = jnp.sum(jnp.where(onehot, before[:, None, :], 0.0), axis=2).astype(jnp.int32)
    return expert_ids * capacity + order_in


def arrange(received, n_expert, exp_dev):
    capacity = received.shape[1]
    width = received.shape[2]
    grouped = received.reshape(n_expert, exp_dev, capacity, width)
    return jnp.transpose(grouped, (1, 0, 2, 3)).reshape(exp_dev, n_expert * capacity, width)


def local_general(grad_out, expert_ids, gate_weights, act, w_down):
    tok_count, top_count = expert_ids.shape
    hidden_slice = act.shape[2]
    exp_dev = w_down.shape[0]
    n_expert = lax.axis_size("expert")
    experts = exp_dev * n_expert
    capacity = 3 * tok_count * top_count // (2 * experts)
    pair_count = tok_count * top_count
    position = slots_of(expert_ids, experts, capacity).reshape(pair_count)
    source = (
        jnp.full((experts * capacity,), pair_count, jnp.int32)
        .at[position]
        .set(jnp.arange(pair_count, dtype=jnp.int32))
    )
    filled = source < pair_count
    token_index = jnp.where(filled, source // top_count, tok_count)
    scaled = (
        (gate_weights[:, :, None] * act.astype(F32)).astype(BF).reshape(pair_count, hidden_slice)
    )
    scaled_ext = jnp.concatenate([scaled, jnp.zeros((1, hidden_slice), BF)], axis=0)
    send_scaled = scaled_ext[jnp.where(filled, source, pair_count)].reshape(
        experts, capacity, hidden_slice
    )
    full_rows = lax.all_gather(grad_out, "section", axis=1, tiled=True)
    rows_ext = jnp.concatenate([full_rows, jnp.zeros((1, full_rows.shape[1]), BF)], axis=0)
    send_grad = rows_ext[token_index].reshape(experts, capacity, full_rows.shape[1])
    recv_grad, recv_scaled = (
        lax.all_to_all(send_grad, "expert", split_axis=0, concat_axis=0, tiled=True),
        lax.all_to_all(send_scaled, "expert", split_axis=0, concat_axis=0, tiled=True),
    )
    recv_grad = arrange(recv_grad, n_expert, exp_dev)
    recv_scaled = arrange(recv_scaled, n_expert, exp_dev)
    unscaled = jnp.einsum("erd,ehd->erh", recv_grad, w_down, preferred_element_type=F32)
    weight_part = jnp.einsum("erh,erd->ehd", recv_scaled, recv_grad, preferred_element_type=F32)
    grad_w = lax.psum_scatter(weight_part.astype(BF), "dp", scatter_dimension=2, tiled=True)
    returning = unscaled.astype(BF).reshape(exp_dev, n_expert, capacity, hidden_slice)
    returning = jnp.transpose(returning, (1, 0, 2, 3)).reshape(experts, capacity, hidden_slice)
    returned = lax.all_to_all(returning, "expert", split_axis=0, concat_axis=0, tiled=True)
    unscaled_tok = returned.reshape(experts * capacity, hidden_slice)[position].reshape(
        tok_count, top_count, hidden_slice
    )
    grad_hidden = (gate_weights[:, :, None] * unscaled_tok.astype(F32)).astype(BF)
    gate_share = jnp.sum(act.astype(F32) * unscaled_tok.astype(F32), axis=2)
    return (grad_hidden, lax.psum(gate_share, "section"), grad_w)


def spread(
    g_ref, ids_ref, g_all, g_half, ids_all, here,
    a_snd, a_rcv, x_snd, x_rcv, y_snd, y_rcv, d_snd, d_rcv, h_snd, h_rcv, i_snd, i_rcv,
):
    dp, sec, z = (lax.axis_index(a) for a in ("dp", "section", "expert"))
    width = g_ref.shape[1]
    half = g_half.shape[2]
    mate = 1 - dp
    sx = sec + 1 - 2 * (sec % 2)
    sy = (sec + 2) % 4
    to_mate, to_x, to_y = (mate, sec, z), (dp, sx, z), (dp, sy, z)
    to_z = [(dp, sec, (z + j) % 4) for j in range(4)]
    other = [(mate, sec, (z + j) % 4) for j in range(4)]
    peers = [to_mate, to_x, to_y] + to_z[1:] + other[1:]

    barrier = pltpu.get_barrier_semaphore()
    for peer in peers:
        pl.semaphore_signal(barrier, inc=1, device_id=peer, device_id_type=MESH)
    pl.semaphore_wait(barrier, len(peers))

    def send(src, dst, snd, rcv, to):
        copy = pltpu.make_async_remote_copy(
            src_ref=src, dst_ref=dst, send_sem=snd, recv_sem=rcv, device_id=to, device_id_type=MESH
        )
        copy.start()
        return copy

    def shard(j, s):
        return g_all.at[j, :, pl.ds(pl.multiple_of(s * width, 128), width)]

    order = (1, 3, 2)
    a = {j: send(g_ref, shard(j, sec), a_snd.at[j], a_rcv.at[j], to_z[j]) for j in order}
    x = {0: send(g_ref, shard(0, sec), x_snd.at[0], x_rcv.at[0], to_x)}
    y = {0: send(g_ref, shard(0, sec), y_snd.at[0], y_rcv.at[0], to_y)}
    own = [
        pltpu.make_async_copy(g_ref, shard(0, sec), here.at[0]),
        pltpu.make_async_copy(ids_ref, ids_all.at[0, 0], here.at[1]),
    ]
    for c in own:
        c.start()
    ids = [send(ids_ref, ids_all.at[1, 0], i_snd.at[1, 0], i_rcv.at[1, 0], to_mate)]
    for j in order:
        ids.append(send(ids_ref, ids_all.at[0, j], i_snd.at[0, j], i_rcv.at[0, j], to_z[j]))
        ids.append(send(ids_ref, ids_all.at[1, j], i_snd.at[1, j], i_rcv.at[1, j], other[j]))

    for j in order:
        a[j].wait_recv()
        x[j] = send(shard(j, sec), shard(j, sec), x_snd.at[j], x_rcv.at[j], to_x)
        y[j] = send(shard(j, sec), shard(j, sec), y_snd.at[j], y_rcv.at[j], to_y)
    d = {}
    for j in (0,) + order:
        if j % 2 == 0:
            x[j].wait_recv()
            d[j] = send(shard(j, sx), shard(j, sx), d_snd.at[j], d_rcv.at[j], to_y)
        else:
            y[j].wait_recv()
            d[j] = send(shard(j, sy), shard(j, sy), d_snd.at[j], d_rcv.at[j], to_x)
    for c in own:
        c.wait()
    h = []
    mate_cols = pl.ds(pl.multiple_of(mate * half, 128), half)
    for j in (0,) + order:
        (y if j % 2 == 0 else x)[j].wait_recv()
        d[j].wait_recv()
        h.append(send(g_all.at[j, :, mate_cols], g_half.at[j], h_snd.at[j], h_rcv.at[j], to_mate))
    for c in ids + h:
        c.wait_recv()
    for c in [*a.values(), *x.values(), *y.values(), *d.values(), *ids, *h]:
        c.wait_send()


VMEM = pl.BlockSpec(memory_space=pltpu.VMEM)


def spread_call(grad_out, ids_t):
    tok_count, width = grad_out.shape
    shapes = (
        jax.ShapeDtypeStruct((4, tok_count, 4 * width), BF),
        jax.ShapeDtypeStruct((4, tok_count, 2 * width), BF),
        jax.ShapeDtypeStruct((2, 4) + ids_t.shape, jnp.int32),
    )
    return pl.pallas_call(
        spread,
        out_shape=shapes,
        in_specs=[VMEM] * 2,
        out_specs=(VMEM,) * 3,
        scratch_shapes=[pltpu.SemaphoreType.DMA((2,))]
        + [pltpu.SemaphoreType.DMA((4,))] * 10
        + [pltpu.SemaphoreType.DMA((2, 4))] * 2,
        compiler_params=pltpu.CompilerParams(
            collective_id=0, has_side_effects=True, vmem_limit_bytes=24 * 2**20
        ),
    )(grad_out, ids_t)


def widen(wide, tight, per_wide, per_tight, flip):
    shape = (tight, wide) if flip else (wide, tight)
    row = lax.broadcasted_iota(jnp.int32, shape, 1 if flip else 0)
    col = lax.broadcasted_iota(jnp.int32, shape, 0 if flip else 1)
    slot = row % per_wide
    same = (slot < per_tight) & (row // per_wide * per_tight + slot == col)
    return jnp.where(same, 1.0, 0.0).astype(BF)


def expand(pick, table, rows, cols, tile):
    @pl.loop(0, cols // tile)
    def _(i):
        at = pl.ds(pl.multiple_of(i * tile, 128), tile)
        rows[:, at] = jnp.dot(pick[...], table[:, at], preferred_element_type=F32).astype(BF)


def hidden_kernel(padded, capacity, pick, g_all, w_ref, out, rows, wide):
    e = pl.program_id(0)

    @pl.when(e == 0)
    def _():
        for s in range(4):
            expand(pick.at[s], g_all.at[s], rows.at[s], g_all.shape[2], 512)

    at = pl.ds(pl.multiple_of(e * padded, padded), padded)
    mine = jnp.concatenate([rows[s, at, :] for s in range(4)], axis=0)
    unscaled = lax.dot_general(
        mine, w_ref[0], (((1,), (1,)), ((), ())), preferred_element_type=F32
    ).astype(BF)
    for s in range(4):
        wide[s, at, :] = unscaled[s * padded : (s + 1) * padded]

    @pl.when(e == pl.num_programs(0) - 1)
    def _():
        tighten = widen(wide.shape[1], out.shape[1], padded, capacity, True)
        for s in range(4):
            out[s] = jnp.dot(tighten, wide[s], preferred_element_type=F32).astype(BF)


def hidden_call(pick, g_all, w_down, capacity):
    exp_dev, hidden, width = w_down.shape
    padded = pick.shape[1] // exp_dev
    return pl.pallas_call(
        functools.partial(hidden_kernel, padded, capacity),
        grid=(exp_dev,),
        out_shape=jax.ShapeDtypeStruct((4, exp_dev * capacity, hidden), BF),
        in_specs=[VMEM, VMEM, pl.BlockSpec((1, hidden, width), lambda e: (e, 0, 0))],
        out_specs=VMEM,
        scratch_shapes=[
            pltpu.VMEM((4, exp_dev * padded, width), BF),
            pltpu.VMEM((4, exp_dev * padded, hidden), BF),
        ],
        compiler_params=pltpu.CompilerParams(vmem_limit_bytes=28 * 2**20),
        cost_estimate=pl.CostEstimate(
            flops=8 * exp_dev * padded * hidden * width, bytes_accessed=w_down.size * 2, transcendentals=0
        ),
    )(pick, g_all, w_down)


def weight_kernel(padded, capacity, dp_ref, pick, g_all, g_half, s_own, s_mate, out, rows, wide):
    e = pl.program_id(0)
    half = g_half.shape[2]

    @pl.when(e == 0)
    def _():
        cols = pl.ds(pl.multiple_of(dp_ref[0] * half, 128), half)
        loosen = widen(wide.shape[1], s_own.shape[1], padded, capacity, False)
        for s in range(4):
            expand(pick.at[0, s], g_all.at[s, :, cols], rows.at[s], half, 256)
            expand(pick.at[1, s], g_half.at[s], rows.at[4 + s], half, 256)
            wide[s] = jnp.dot(loosen, s_own[s], preferred_element_type=F32).astype(BF)
            wide[4 + s] = jnp.dot(loosen, s_mate[s], preferred_element_type=F32).astype(BF)

    at = pl.ds(pl.multiple_of(e * padded, padded), padded)
    grads = jnp.concatenate([rows[s, at, :] for s in range(8)], axis=0)
    scaled = jnp.concatenate([wide[s, at, :] for s in range(8)], axis=0)
    out[0] = lax.dot_general(
        scaled, grads, (((0,), (0,)), ((), ())), preferred_element_type=F32
    ).astype(BF)


def weight_call(dp, pick, g_all, g_half, s_own, s_mate, exp_dev, capacity):
    padded = pick.shape[2] // exp_dev
    half, hidden = g_half.shape[2], s_own.shape[2]
    return pl.pallas_call(
        functools.partial(weight_kernel, padded, capacity),
        grid=(exp_dev,),
        out_shape=jax.ShapeDtypeStruct((exp_dev, hidden, half), BF),
        in_specs=[pl.BlockSpec(memory_space=pltpu.SMEM)] + [VMEM] * 5,
        out_specs=pl.BlockSpec((1, hidden, half), lambda e: (e, 0, 0)),
        scratch_shapes=[
            pltpu.VMEM((8, exp_dev * padded, half), BF),
            pltpu.VMEM((8, exp_dev * padded, hidden), BF),
        ],
        compiler_params=pltpu.CompilerParams(vmem_limit_bytes=28 * 2**20),
        cost_estimate=pl.CostEstimate(
            flops=16 * exp_dev * padded * hidden * half, bytes_accessed=exp_dev * hidden * half * 2, transcendentals=0
        ),
    )(dp, pick, g_all, g_half, s_own, s_mate)


def local(grad_out, expert_ids, gate_weights, act, w_down):
    tok_count, top_count = expert_ids.shape
    hidden = act.shape[2]
    exp_dev = w_down.shape[0]
    experts = exp_dev * 4
    capacity = 3 * tok_count * top_count // (2 * experts)
    padded = -(-capacity // 32) * 32
    pairs = tok_count * top_count
    per_dev = exp_dev * capacity
    dp, z = lax.axis_index("dp"), lax.axis_index("expert")

    g_all, g_half, ids_all = spread_call(grad_out, expert_ids.T)

    first = expert_ids - z * exp_dev
    first = jnp.where(first < 0, first + experts, first)
    position = slots_of(first, experts, capacity).reshape(pairs)
    scaled = (gate_weights[:, :, None] * act.astype(F32)).astype(BF).reshape(pairs, hidden)
    slots = jnp.arange(experts * capacity, dtype=jnp.int32)
    place = (slots[:, None] == position[None, :]).astype(BF)
    send_scaled = jnp.dot(place, scaled, preferred_element_type=F32).astype(BF)
    send_scaled = send_scaled.reshape(4, per_dev, hidden)
    send_scaled, g_all, ids_all = lax.optimization_barrier((send_scaled, g_all, ids_all))
    s_own = [
        lax.ppermute(send_scaled[j], "expert", [(i, (i + j) % 4) for i in range(4)])
        if j
        else send_scaled[0]
        for j in range(4)
    ]

    mine = z * exp_dev + jnp.arange(exp_dev, dtype=jnp.int32)
    named = jnp.any(ids_all[:, :, None] == mine[None, None, :, None, None], axis=3)
    earlier = jnp.arange(tok_count)[:, None] < jnp.arange(tok_count)[None, :]
    before = jnp.einsum(
        "rseu,ut->rset", named.astype(BF), earlier.astype(BF), preferred_element_type=F32
    ).astype(jnp.int32)
    before = jnp.where(named, before, -1)
    pick = (before[:, :, :, None, :] == jnp.arange(padded)[:, None]).astype(BF)
    pick = pick.reshape(2, 4, exp_dev * padded, tok_count)

    returning = hidden_call(pick[0], g_all, w_down, capacity)
    s_own, returning = lax.optimization_barrier((s_own, returning))
    s_own = jnp.stack(s_own)
    s_mate = lax.ppermute(s_own, "dp", [(0, 1), (1, 0)])
    back = [
        lax.ppermute(returning[j], "expert", [(i, (i - j) % 4) for i in range(4)])
        if j
        else returning[0]
        for j in range(4)
    ]
    grad_w = weight_call(
        dp.astype(jnp.int32).reshape(1), pick, g_all, g_half, s_own, s_mate, exp_dev, capacity
    )

    back, grad_w = lax.optimization_barrier((back, grad_w))
    fetch = (position[:, None] == slots[None, :]).astype(BF)
    unscaled_tok = jnp.dot(fetch, jnp.concatenate(back, axis=0), preferred_element_type=F32)
    unscaled_tok = unscaled_tok.reshape(tok_count, top_count, hidden)
    grad_hidden = (gate_weights[:, :, None] * unscaled_tok).astype(BF)
    share = jnp.sum(act.astype(F32) * unscaled_tok, axis=2)
    other = [lax.ppermute(share, "section", [(i, i ^ m) for i in range(4)]) for m in (1, 2, 3)]
    return (grad_hidden, (share + other[0]) + (other[1] + other[2]), grad_w)


def solution(mesh):
    placed = (
        P(("dp", "expert"), "section"),
        P(("dp", "expert"), None),
        P(("dp", "expert"), None),
        P(("dp", "expert"), None, "section"),
        P("expert", "section", None),
    )
    sizes = tuple(mesh.shape[a] for a in ("dp", "section", "expert"))
    return jax.shard_map(
        local if sizes == (2, 4, 4) else local_general,
        mesh=mesh,
        in_specs=placed,
        out_specs=(
            P(("dp", "expert"), None, "section"),
            P(("dp", "expert"), None),
            P("expert", "section", "dp"),
        ),
        check_vma=False,
    )
```

```python
import functools

import jax
import jax.numpy as jnp
from jax import lax
from jax.experimental import pallas as pl
from jax.experimental.pallas import tpu as pltpu
from jax.sharding import PartitionSpec as P

BF = jnp.bfloat16
F32 = jnp.float32
MESH = pl.DeviceIdType.MESH


def slots_of(expert_ids, experts, capacity):
    tok_count = expert_ids.shape[0]
    onehot = expert_ids[:, :, None] == jnp.arange(experts, dtype=jnp.int32)
    named = jnp.any(onehot, axis=1).astype(BF)
    earlier = jnp.arange(tok_count)[:, None] > jnp.arange(tok_count)[None, :]
    before = jnp.dot(earlier.astype(BF), named, preferred_element_type=F32)
    order_in = jnp.sum(jnp.where(onehot, before[:, None, :], 0.0), axis=2).astype(jnp.int32)
    return expert_ids * capacity + order_in


def arrange(received, n_expert, exp_dev):
    capacity = received.shape[1]
    width = received.shape[2]
    grouped = received.reshape(n_expert, exp_dev, capacity, width)
    return jnp.transpose(grouped, (1, 0, 2, 3)).reshape(exp_dev, n_expert * capacity, width)


def local_general(grad_out, expert_ids, gate_weights, act, w_down):
    tok_count, top_count = expert_ids.shape
    hidden_slice = act.shape[2]
    exp_dev = w_down.shape[0]
    n_expert = lax.axis_size("expert")
    experts = exp_dev * n_expert
    capacity = 3 * tok_count * top_count // (2 * experts)
    pair_count = tok_count * top_count
    position = slots_of(expert_ids, experts, capacity).reshape(pair_count)
    source = (
        jnp.full((experts * capacity,), pair_count, jnp.int32)
        .at[position]
        .set(jnp.arange(pair_count, dtype=jnp.int32))
    )
    filled = source < pair_count
    token_index = jnp.where(filled, source // top_count, tok_count)
    scaled = (
        (gate_weights[:, :, None] * act.astype(F32)).astype(BF).reshape(pair_count, hidden_slice)
    )
    scaled_ext = jnp.concatenate([scaled, jnp.zeros((1, hidden_slice), BF)], axis=0)
    send_scaled = scaled_ext[jnp.where(filled, source, pair_count)].reshape(
        experts, capacity, hidden_slice
    )
    full_rows = lax.all_gather(grad_out, "section", axis=1, tiled=True)
    rows_ext = jnp.concatenate([full_rows, jnp.zeros((1, full_rows.shape[1]), BF)], axis=0)
    send_grad = rows_ext[token_index].reshape(experts, capacity, full_rows.shape[1])
    recv_grad, recv_scaled = (
        lax.all_to_all(send_grad, "expert", split_axis=0, concat_axis=0, tiled=True),
        lax.all_to_all(send_scaled, "expert", split_axis=0, concat_axis=0, tiled=True),
    )
    recv_grad = arrange(recv_grad, n_expert, exp_dev)
    recv_scaled = arrange(recv_scaled, n_expert, exp_dev)
    unscaled = jnp.einsum("erd,ehd->erh", recv_grad, w_down, preferred_element_type=F32)
    weight_part = jnp.einsum("erh,erd->ehd", recv_scaled, recv_grad, preferred_element_type=F32)
    grad_w = lax.psum_scatter(weight_part.astype(BF), "dp", scatter_dimension=2, tiled=True)
    returning = unscaled.astype(BF).reshape(exp_dev, n_expert, capacity, hidden_slice)
    returning = jnp.transpose(returning, (1, 0, 2, 3)).reshape(experts, capacity, hidden_slice)
    returned = lax.all_to_all(returning, "expert", split_axis=0, concat_axis=0, tiled=True)
    unscaled_tok = returned.reshape(experts * capacity, hidden_slice)[position].reshape(
        tok_count, top_count, hidden_slice
    )
    grad_hidden = (gate_weights[:, :, None] * unscaled_tok.astype(F32)).astype(BF)
    gate_share = jnp.sum(act.astype(F32) * unscaled_tok.astype(F32), axis=2)
    return (grad_hidden, lax.psum(gate_share, "section"), grad_w)


def spread(
    g_ref, ids_ref, g_all, g_half, ids_all, here,
    a_snd, a_rcv, x_snd, x_rcv, y_snd, y_rcv, d_snd, d_rcv, h_snd, h_rcv, i_snd, i_rcv,
):
    dp, sec, z = (lax.axis_index(a) for a in ("dp", "section", "expert"))
    width = g_ref.shape[1]
    half = g_half.shape[2]
    mate = 1 - dp
    sx = sec + 1 - 2 * (sec % 2)
    sy = (sec + 2) % 4
    to_mate, to_x, to_y = (mate, sec, z), (dp, sx, z), (dp, sy, z)
    to_z = [(dp, sec, (z + j) % 4) for j in range(4)]
    other = [(mate, sec, (z + j) % 4) for j in range(4)]
    peers = [to_mate, to_x, to_y] + to_z[1:] + other[1:]

    barrier = pltpu.get_barrier_semaphore()
    for peer in peers:
        pl.semaphore_signal(barrier, inc=1, device_id=peer, device_id_type=MESH)
    pl.semaphore_wait(barrier, len(peers))

    def send(src, dst, snd, rcv, to):
        copy = pltpu.make_async_remote_copy(
            src_ref=src, dst_ref=dst, send_sem=snd, recv_sem=rcv, device_id=to, device_id_type=MESH
        )
        copy.start()
        return copy

    def shard(j, s):
        return g_all.at[j, :, pl.ds(pl.multiple_of(s * width, 128), width)]

    order = (1, 3, 2)
    a = {j: send(g_ref, shard(j, sec), a_snd.at[j], a_rcv.at[j], to_z[j]) for j in order}
    x = {0: send(g_ref, shard(0, sec), x_snd.at[0], x_rcv.at[0], to_x)}
    y = {0: send(g_ref, shard(0, sec), y_snd.at[0], y_rcv.at[0], to_y)}
    own = [
        pltpu.make_async_copy(g_ref, shard(0, sec), here.at[0]),
        pltpu.make_async_copy(ids_ref, ids_all.at[0, 0], here.at[1]),
    ]
    for c in own:
        c.start()
    ids = [send(ids_ref, ids_all.at[1, 0], i_snd.at[1, 0], i_rcv.at[1, 0], to_mate)]
    for j in order:
        ids.append(send(ids_ref, ids_all.at[0, j], i_snd.at[0, j], i_rcv.at[0, j], to_z[j]))
        ids.append(send(ids_ref, ids_all.at[1, j], i_snd.at[1, j], i_rcv.at[1, j], other[j]))

    d, h = {}, []
    mate_cols = pl.ds(pl.multiple_of(mate * half, 128), half)

    def relay(j):
        if j % 2 == 0:
            x[j].wait_recv()
            d[j] = send(shard(j, sx), shard(j, sx), d_snd.at[j], d_rcv.at[j], to_y)
        else:
            y[j].wait_recv()
            d[j] = send(shard(j, sy), shard(j, sy), d_snd.at[j], d_rcv.at[j], to_x)

    def pass_half(j):
        (y if j % 2 == 0 else x)[j].wait_recv()
        d[j].wait_recv()
        h.append(send(g_all.at[j, :, mate_cols], g_half.at[j], h_snd.at[j], h_rcv.at[j], to_mate))

    def onward(j):
        a[j].wait_recv()
        x[j] = send(shard(j, sec), shard(j, sec), x_snd.at[j], x_rcv.at[j], to_x)
        y[j] = send(shard(j, sec), shard(j, sec), y_snd.at[j], y_rcv.at[j], to_y)

    relay(0)
    onward(1)
    onward(3)
    relay(1)
    relay(3)
    onward(2)
    for c in own:
        c.wait()
    pass_half(0)
    relay(2)
    for j in order:
        pass_half(j)
    for c in ids + h:
        c.wait_recv()
    for c in [*a.values(), *x.values(), *y.values(), *d.values(), *ids, *h]:
        c.wait_send()


VMEM = pl.BlockSpec(memory_space=pltpu.VMEM)


def spread_call(grad_out, ids_t):
    tok_count, width = grad_out.shape
    shapes = (
        jax.ShapeDtypeStruct((4, tok_count, 4 * width), BF),
        jax.ShapeDtypeStruct((4, tok_count, 2 * width), BF),
        jax.ShapeDtypeStruct((2, 4) + ids_t.shape, jnp.int32),
    )
    return pl.pallas_call(
        spread,
        out_shape=shapes,
        in_specs=[VMEM] * 2,
        out_specs=(VMEM,) * 3,
        scratch_shapes=[pltpu.SemaphoreType.DMA((2,))]
        + [pltpu.SemaphoreType.DMA((4,))] * 10
        + [pltpu.SemaphoreType.DMA((2, 4))] * 2,
        compiler_params=pltpu.CompilerParams(
            collective_id=0, has_side_effects=True, vmem_limit_bytes=24 * 2**20
        ),
    )(grad_out, ids_t)


def widen(wide, tight, per_wide, per_tight, flip):
    shape = (tight, wide) if flip else (wide, tight)
    row = lax.broadcasted_iota(jnp.int32, shape, 1 if flip else 0)
    col = lax.broadcasted_iota(jnp.int32, shape, 0 if flip else 1)
    slot = row % per_wide
    same = (slot < per_tight) & (row // per_wide * per_tight + slot == col)
    return jnp.where(same, 1.0, 0.0).astype(BF)


def expand(pick, table, rows, cols, tile):
    @pl.loop(0, cols // tile)
    def _(i):
        at = pl.ds(pl.multiple_of(i * tile, 128), tile)
        rows[:, at] = jnp.dot(pick[...], table[:, at], preferred_element_type=F32).astype(BF)


def hidden_kernel(padded, capacity, pick, g_all, w_ref, out, rows, wide):
    e = pl.program_id(0)

    @pl.when(e == 0)
    def _():
        for s in range(4):
            expand(pick.at[s], g_all.at[s], rows.at[s], g_all.shape[2], 512)

    at = pl.ds(pl.multiple_of(e * padded, padded), padded)
    mine = jnp.concatenate([rows[s, at, :] for s in range(4)], axis=0)
    unscaled = lax.dot_general(
        mine, w_ref[0], (((1,), (1,)), ((), ())), preferred_element_type=F32
    ).astype(BF)
    for s in range(4):
        wide[s, at, :] = unscaled[s * padded : (s + 1) * padded]

    @pl.when(e == pl.num_programs(0) - 1)
    def _():
        tighten = widen(wide.shape[1], out.shape[1], padded, capacity, True)
        for s in range(4):
            out[s] = jnp.dot(tighten, wide[s], preferred_element_type=F32).astype(BF)


def hidden_call(pick, g_all, w_down, capacity):
    exp_dev, hidden, width = w_down.shape
    padded = pick.shape[1] // exp_dev
    return pl.pallas_call(
        functools.partial(hidden_kernel, padded, capacity),
        grid=(exp_dev,),
        out_shape=jax.ShapeDtypeStruct((4, exp_dev * capacity, hidden), BF),
        in_specs=[VMEM, VMEM, pl.BlockSpec((1, hidden, width), lambda e: (e, 0, 0))],
        out_specs=VMEM,
        scratch_shapes=[
            pltpu.VMEM((4, exp_dev * padded, width), BF),
            pltpu.VMEM((4, exp_dev * padded, hidden), BF),
        ],
        compiler_params=pltpu.CompilerParams(vmem_limit_bytes=28 * 2**20),
        cost_estimate=pl.CostEstimate(
            flops=8 * exp_dev * padded * hidden * width, bytes_accessed=w_down.size * 2, transcendentals=0
        ),
    )(pick, g_all, w_down)


def weight_kernel(padded, capacity, dp_ref, pick, g_all, g_half, s_own, s_mate, out, rows, wide):
    e = pl.program_id(0)
    half = g_half.shape[2]

    @pl.when(e == 0)
    def _():
        cols = pl.ds(pl.multiple_of(dp_ref[0] * half, 128), half)
        loosen = widen(wide.shape[1], s_own.shape[1], padded, capacity, False)
        for s in range(4):
            expand(pick.at[0, s], g_all.at[s, :, cols], rows.at[s], half, 256)
            expand(pick.at[1, s], g_half.at[s], rows.at[4 + s], half, 256)
            wide[s] = jnp.dot(loosen, s_own[s], preferred_element_type=F32).astype(BF)
            wide[4 + s] = jnp.dot(loosen, s_mate[s], preferred_element_type=F32).astype(BF)

    at = pl.ds(pl.multiple_of(e * padded, padded), padded)
    grads = jnp.concatenate([rows[s, at, :] for s in range(8)], axis=0)
    scaled = jnp.concatenate([wide[s, at, :] for s in range(8)], axis=0)
    out[0] = lax.dot_general(
        scaled, grads, (((0,), (0,)), ((), ())), preferred_element_type=F32
    ).astype(BF)


def weight_call(dp, pick, g_all, g_half, s_own, s_mate, exp_dev, capacity):
    padded = pick.shape[2] // exp_dev
    half, hidden = g_half.shape[2], s_own.shape[2]
    return pl.pallas_call(
        functools.partial(weight_kernel, padded, capacity),
        grid=(exp_dev,),
        out_shape=jax.ShapeDtypeStruct((exp_dev, hidden, half), BF),
        in_specs=[pl.BlockSpec(memory_space=pltpu.SMEM)] + [VMEM] * 5,
        out_specs=pl.BlockSpec((1, hidden, half), lambda e: (e, 0, 0)),
        scratch_shapes=[
            pltpu.VMEM((8, exp_dev * padded, half), BF),
            pltpu.VMEM((8, exp_dev * padded, hidden), BF),
        ],
        compiler_params=pltpu.CompilerParams(vmem_limit_bytes=28 * 2**20),
        cost_estimate=pl.CostEstimate(
            flops=16 * exp_dev * padded * hidden * half, bytes_accessed=exp_dev * hidden * half * 2, transcendentals=0
        ),
    )(dp, pick, g_all, g_half, s_own, s_mate)


def local(grad_out, expert_ids, gate_weights, act, w_down):
    tok_count, top_count = expert_ids.shape
    hidden = act.shape[2]
    exp_dev = w_down.shape[0]
    experts = exp_dev * 4
    capacity = 3 * tok_count * top_count // (2 * experts)
    padded = -(-capacity // 32) * 32
    pairs = tok_count * top_count
    per_dev = exp_dev * capacity
    dp, z = lax.axis_index("dp"), lax.axis_index("expert")

    g_all, g_half, ids_all = spread_call(grad_out, expert_ids.T)

    first = expert_ids - z * exp_dev
    first = jnp.where(first < 0, first + experts, first)
    position = slots_of(first, experts, capacity).reshape(pairs)
    scaled = (gate_weights[:, :, None] * act.astype(F32)).astype(BF).reshape(pairs, hidden)
    slots = jnp.arange(experts * capacity, dtype=jnp.int32)
    place = (slots[:, None] == position[None, :]).astype(BF)
    send_scaled = jnp.dot(place, scaled, preferred_element_type=F32).astype(BF)
    send_scaled = send_scaled.reshape(4, per_dev, hidden)
    send_scaled, g_all, ids_all = lax.optimization_barrier((send_scaled, g_all, ids_all))
    s_own = [
        lax.ppermute(send_scaled[j], "expert", [(i, (i + j) % 4) for i in range(4)])
        if j
        else send_scaled[0]
        for j in range(4)
    ]

    mine = z * exp_dev + jnp.arange(exp_dev, dtype=jnp.int32)
    named = jnp.any(ids_all[:, :, None] == mine[None, None, :, None, None], axis=3)
    earlier = jnp.arange(tok_count)[:, None] < jnp.arange(tok_count)[None, :]
    before = jnp.einsum(
        "rseu,ut->rset", named.astype(BF), earlier.astype(BF), preferred_element_type=F32
    ).astype(jnp.int32)
    before = jnp.where(named, before, -1)
    pick = (before[:, :, :, None, :] == jnp.arange(padded)[:, None]).astype(BF)
    pick = pick.reshape(2, 4, exp_dev * padded, tok_count)

    returning = hidden_call(pick[0], g_all, w_down, capacity)
    s_own, returning = lax.optimization_barrier((s_own, returning))
    s_own = jnp.stack(s_own)
    s_mate = lax.ppermute(s_own, "dp", [(0, 1), (1, 0)])
    back = [
        lax.ppermute(returning[j], "expert", [(i, (i - j) % 4) for i in range(4)])
        if j
        else returning[0]
        for j in range(4)
    ]
    grad_w = weight_call(
        dp.astype(jnp.int32).reshape(1), pick, g_all, g_half, s_own, s_mate, exp_dev, capacity
    )

    back, grad_w = lax.optimization_barrier((back, grad_w))
    fetch = (position[:, None] == slots[None, :]).astype(BF)
    unscaled_tok = jnp.dot(fetch, jnp.concatenate(back, axis=0), preferred_element_type=F32)
    unscaled_tok = unscaled_tok.reshape(tok_count, top_count, hidden)
    grad_hidden = (gate_weights[:, :, None] * unscaled_tok).astype(BF)
    share = jnp.sum(act.astype(F32) * unscaled_tok, axis=2)
    other = [lax.ppermute(share, "section", [(i, i ^ m) for i in range(4)]) for m in (1, 2, 3)]
    return (grad_hidden, (share + other[0]) + (other[1] + other[2]), grad_w)


def solution(mesh):
    placed = (
        P(("dp", "expert"), "section"),
        P(("dp", "expert"), None),
        P(("dp", "expert"), None),
        P(("dp", "expert"), None, "section"),
        P("expert", "section", None),
    )
    sizes = tuple(mesh.shape[a] for a in ("dp", "section", "expert"))
    return jax.shard_map(
        local if sizes == (2, 4, 4) else local_general,
        mesh=mesh,
        in_specs=placed,
        out_specs=(
            P(("dp", "expert"), None, "section"),
            P(("dp", "expert"), None),
            P("expert", "section", "dp"),
        ),
        check_vma=False,
    )
```
